128 devices in a mesh: dp: 8 (over z, x_lo), mp: 16 (over y, x_hi, core).
Axes of the slice: x: 4 (x_hi: 2, x_lo: 2; x = x_hi * 2 + x_lo), y: 4, z: 4, core: 2. Of those that a mesh axis runs over, the one named last changes fastest.
Arguments:
- activations: bfloat16 [8192, 4096], P('dp', 'mp'), may hold values from -6 to 6
- cotangent: bfloat16 [8192, 16384], P('dp', 'mp'), may hold values from -0.15625 to 0.15625
- weight: float32 [4096, 16384], P('dp', 'mp'), may hold values from -6 to 6
- stat_prev: float32 [16, 8, 1024, 1024], P('mp', 'dp'), may hold values from -143360 to 143360, as said below
- assignment: int32 [16, 8], P('mp', 'dp'), may hold values from 0 to 7, each once within a row
- left_stale: bfloat16 [16, 4096, 1024], P('mp', 'dp'), may hold values from -0.1875 to 0.1875
- right_stale: bfloat16 [16, 4, 1024, 1024], P('mp'), may hold values from -0.1875 to 0.1875
Outputs:
- new_weight: float32 [4096, 16384], P('dp', 'mp')
- new_stat: float32 [16, 8, 1024, 1024], P('mp', 'dp')
- fresh_root: float32 [16, 8, 1024, 1024], P('mp', 'dp')
The draws below stay inside these ranges and needn't reach their ends.
Inputs may be any that keep to these rules, and one draw needn't show every extreme that they name: Each [1024, 1024] matrix of stat_prev is symmetric and positive definite. Each row of assignment holds every number of 0 to 7 once.
All inputs are finite; a program needn't handle non-finite values.
Results may differ from the reference program's by a relative error of at most 0.0085.
Values may be sent and summed in bfloat16 or wider, within the bound.
No kernel may reach another device: no remote copies, remote signals or barrier semaphores. Data moves between devices by JAX's collectives and lax.ppermute only.
A program may use at most 128 MiB of HBM per device.

```python
import math
import jax
import jax.numpy as jnp
from jax import lax

BLK = 1024
RB = 4
ITERS = 2
TOK_DEV = 1024
DIN = 4096
NCOL = 16
DOUT = 16384
TOKENS = 8192
PROBS = 8
N_DP = 8


def draw_stat_prev(key, part):
    key = jax.random.fold_in(key, 11)
    key_basis = jax.random.fold_in(key, 1)
    key_spread = jax.random.fold_in(key, 2)
    key_ridge = jax.random.fold_in(key, 3)
    root_three = math.sqrt(3.0)
    basis = jax.random.uniform(key_basis, (NCOL, PROBS, BLK, BLK), jnp.float32, -root_three, root_three)
    spread = jnp.exp(jax.random.uniform(key_spread, (NCOL, PROBS, BLK), jnp.float32, math.log(0.05), math.log(5.0)))
    dense = jnp.einsum('cpik,cpjk->cpij', basis * spread[:, :, None, :], basis, precision=lax.Precision.HIGHEST)
    dense = 0.5 * (dense + jnp.swapaxes(dense, -1, -2))
    ridge = jax.random.uniform(key_ridge, (NCOL, PROBS, BLK), jnp.float32, 0.05, 0.2) * BLK
    identity = jnp.eye(BLK, dtype=jnp.float32)
    statistic = dense + ridge[..., None] * identity
    return statistic


def level_of(key, extent, cuts, least, largest):
    gain = 1.0
    for dim, shards_of in cuts:
        heights = jax.random.uniform(jax.random.fold_in(jax.random.fold_in(key, 6), dim), (shards_of,), jnp.float32, least / len(cuts), largest / len(cuts))
        gain = gain * jnp.repeat(jnp.exp(heights), extent[dim] // shards_of).reshape((-1,) + (1,) * (len(extent) - 1 - dim))
    return gain


def normal_values(rng, shape, width, reach, split=(), kind=jnp.bfloat16):
    values = jax.random.normal(rng, shape, jnp.float32) * width
    if len(split) > 0:
        values = level_of(rng, shape, split, -0.22, 0.18) * values
    return jnp.clip(values, min=-reach, max=reach).astype(kind)


def setup_inputs(seed: int = 0) -> dict:
    splits = jax.random.split(jax.random.key(seed), 8)
    return {
        "activations": normal_values(splits[0], (TOKENS, DIN), 1.0, 6.0, ((0, 8), (1, 16))),
        "cotangent": normal_values(splits[1], (TOKENS, DOUT), (TOKENS ** -0.5), 0.15625, ((0, 8), (1, 16))),
        "weight": normal_values(splits[2], (DIN, DOUT), 1.0, 6.0, ((0, 8), (1, 16)), jnp.float32),
        "stat_prev": draw_stat_prev(jax.random.fold_in(splits[7], 71), 0),
        "assignment": jax.vmap(lambda own: jax.random.permutation(own, PROBS))(jax.random.split(splits[4], NCOL)).reshape((NCOL, PROBS)).astype(jnp.int32),
        "left_stale": normal_values(splits[5], (NCOL, DIN, BLK), BLK ** -0.5, 0.1875, ((0, 16), (1, 8))),
        "right_stale": normal_values(splits[6], (NCOL, RB, BLK, BLK), BLK ** -0.5, 0.1875, ((0, 16),)),
    }


def matmul_high(left, right):
    return jnp.dot(left, right, precision=lax.Precision.HIGHEST, preferred_element_type=jnp.float32)


def newton_root(statistic):
    norm_scale = 2.0 * jnp.sum(statistic * statistic) / jnp.trace(statistic)
    identity = jnp.eye(BLK, dtype=jnp.float32)
    normed = statistic / norm_scale
    inverse_root = identity
    for iteration in range(ITERS):
        factor = (5.0 * identity - normed) * 0.25
        if iteration == 0:
            inverse_root = factor
        else:
            inverse_root = matmul_high(inverse_root, factor)
        if iteration + 1 < ITERS:
            square = matmul_high(factor, factor)
            normed = matmul_high(square, matmul_high(square, normed))
    return inverse_root * norm_scale ** -0.25


def gram_stat(gradient, column_start, problem, previous):
    block_index = jnp.where(problem < RB, problem, problem - RB)
    grad_tile = lax.dynamic_slice(gradient, (block_index * BLK, column_start), (BLK, BLK))
    oriented = jnp.where(problem < RB, grad_tile, grad_tile.T)
    gram = jnp.dot(oriented, oriented.T, preferred_element_type=jnp.float32)
    statistic = previous + gram
    return statistic, newton_root(statistic)


def reference(activations, cotangent, weight, stat_prev, assignment, left_stale, right_stale):
    act_groups = activations.reshape(N_DP, TOK_DEV, DIN)
    cot_groups = cotangent.reshape(N_DP, TOK_DEV, DOUT)

    def accumulate(running, operands):
        group_acts, group_cots = operands
        partial_value = lax.dot_general(group_acts, group_cots, (((0,), (0,)), ((), ())), preferred_element_type=jnp.float32)
        rounded = lax.optimization_barrier(partial_value.astype(jnp.bfloat16))
        return running + rounded.astype(jnp.float32), None

    running, unused = lax.scan(accumulate, jnp.zeros((DIN, DOUT), jnp.float32), (act_groups, cot_groups))
    gradient = running.astype(jnp.bfloat16)
    column_starts = jnp.repeat(jnp.arange(NCOL, dtype=jnp.int32), PROBS) * BLK

    def solve_one(operands):
        column_start, problem, previous = operands
        return gram_stat(gradient, column_start, problem, previous)

    new_stat, fresh_root = lax.map(solve_one, (column_starts, assignment.reshape(-1), stat_prev.reshape(NCOL * PROBS, BLK, BLK)))
    new_stat = new_stat.reshape(NCOL, PROBS, BLK, BLK)
    fresh_root = fresh_root.reshape(NCOL, PROBS, BLK, BLK)
    updated = []
    for column in range(NCOL):
        left_blocks = left_stale[column].reshape(RB, BLK, BLK).astype(jnp.float32)
        grad_blocks = gradient[:, column * BLK:(column + 1) * BLK].reshape(RB, BLK, BLK).astype(jnp.float32)
        applied = jnp.einsum("rij,rjk->rik", left_blocks, grad_blocks, precision=lax.Precision.HIGHEST)
        applied = lax.optimization_barrier(applied.astype(jnp.bfloat16)).astype(jnp.float32)
        update = jnp.einsum("rij,rjk->rik", applied, right_stale[column].astype(jnp.float32), precision=lax.Precision.HIGHEST)
        updated.append(weight[:, column * BLK:(column + 1) * BLK] - 0.5 * update.reshape(DIN, BLK))
    new_weight = jnp.concatenate(updated, axis=1)
    return new_weight, new_stat, fresh_root
```

```python
import jax
import jax.numpy as jnp
from jax import lax
from jax.sharding import Mesh, PartitionSpec as P

BLK = 1024
RB = 4
CHUNKS = 2
COLS = BLK // CHUNKS
BF = jnp.bfloat16
F32 = jnp.float32


def ring(step):
    return [(i, (i + step) % 4) for i in range(4)]


SWAP = [(0, 1), (1, 0)]


def x_index(x):
    return (x % 2) * 2 + x // 2


def x_perm(pairs):
    return [(x_index(s), x_index(d)) for s, d in pairs]


def add(first, *others):
    total = first.astype(F32)
    for other in others:
        total = total + other.astype(F32)
    return total.astype(BF)


def z_reduce(part, z):
    def block(offset):
        return lax.dynamic_index_in_dim(part, (z + offset) % 4, 0, keepdims=False)

    far = block(2)
    up = lax.ppermute(far[:256], "z", ring(1))
    down = lax.ppermute(far[256:], "z", ring(-1))
    nxt = block(1)
    prv = block(3)
    nxt = jnp.concatenate([add(nxt[:256], up), nxt[256:]], 0)
    prv = jnp.concatenate([prv[:256], add(prv[256:], down)], 0)
    from_prv = lax.ppermute(nxt, "z", ring(1))
    from_nxt = lax.ppermute(prv, "z", ring(-1))
    own = add(block(0), from_prv, from_nxt)
    got_prv = lax.ppermute(own, "z", ring(1))
    got_nxt = lax.ppermute(own, "z", ring(-1))
    far_a = lax.ppermute(got_prv[:256], "z", ring(1))
    far_b = lax.ppermute(got_nxt[256:], "z", ring(-1))
    return [own, got_nxt, jnp.concatenate([far_a, far_b], 0), got_prv]


def mm(left, right, precision):
    return jnp.dot(left, right, precision=precision, preferred_element_type=F32)


def newton_root(statistic):
    norm_scale = 2.0 * jnp.sum(statistic * statistic) / jnp.trace(statistic)
    eye = jnp.eye(BLK, dtype=F32)
    high = lax.Precision.HIGH
    m = statistic / norm_scale
    m2 = mm(m, m, high)
    e = (m2 - 10.0 * m) * 0.0625
    mf = (5.0 * m - m2) * 0.25
    base = 25.0 / 16.0
    w = 2.0 * base * e + mm(e, e, high)
    prod = base * base * mf + mm(w, mf, high)
    root = (5.0 * (5.0 * eye - m) * 0.25 - prod) * 0.25
    return root * norm_scale ** (-0.25)


def on_device(activations, cotangent, weight, stat_prev, assignment, left_stale, right_stale):
    z = lax.axis_index("z")
    xl = lax.axis_index("xl")
    y = lax.axis_index("y")
    xh = lax.axis_index("xh")
    core = lax.axis_index("core")
    half = xl ^ xh

    recv_mine = lax.ppermute(activations, ("xl", "xh"), x_perm([(1, 3), (3, 1)]))
    other = lax.ppermute(activations, ("xl", "xh"), x_perm([(1, 0), (3, 2), (0, 3), (2, 1)]))
    mine = jnp.where(xl == 0, activations, recv_mine)
    feats = jnp.concatenate([mine, other], 0)
    from_below = lax.ppermute(feats, "y", ring(1))
    from_above = lax.ppermute(feats, "y", ring(-1))
    far_a = lax.ppermute(from_below[:BLK], "y", ring(1))
    far_b = lax.ppermute(from_above[BLK:], "y", ring(-1))
    far = jnp.concatenate([far_a, far_b], 0)
    tiles = []
    for own in (feats, from_above, far, from_below):
        tiles += [own, lax.ppermute(own, "core", SWAP)]
    lhs = jnp.concatenate(tiles, 1)

    problem = assignment[0, 0]
    partner_problem = lax.ppermute(assignment, "xl", SWAP)[0, 0]

    gram_mine, gram_other, upd_mine, upd_other = [], [], [], []
    for chunk in range(CHUNKS):
        own_cot = cotangent[:, chunk * COLS:(chunk + 1) * COLS]
        rhs = jnp.concatenate([own_cot, lax.ppermute(own_cot, "xl", SWAP)], 0)
        part = lax.dot_general(lhs, rhs, (((0,), (0,)), ((), ())), preferred_element_type=F32).astype(BF)
        blocks = z_reduce(part.reshape(4, 512, COLS), z)

        def pick(tile):
            which = (tile - y - z) % 4
            return lax.select_n(which, *blocks)

        gram_mine.append(pick(problem % RB))
        gram_other.append(lax.ppermute(pick(partner_problem % RB), "xl", SWAP))
        mine_u = pick(z)
        upd_mine.append(mine_u)
        upd_other.append(lax.ppermute(mine_u, "xl", SWAP))

    def assemble(mine_parts, other_parts):
        whole = jnp.stack([jnp.concatenate(mine_parts, 1), jnp.concatenate(other_parts, 1)], 0).reshape(2, 2, 256, BLK)
        whole = jnp.where(half == 0, whole, whole[::-1])
        whole = jnp.where(core == 0, whole, whole[:, ::-1])
        return whole.reshape(BLK, BLK)

    tile = assemble(gram_mine, gram_other)
    oriented = jnp.where(problem < RB, tile, tile.T)
    gram = jnp.dot(oriented, oriented.T, preferred_element_type=F32)
    new_stat = stat_prev[0, 0] + gram
    root = newton_root(new_stat)

    upd_tile = assemble(upd_mine, upd_other)
    applied = jnp.dot(left_stale[0], upd_tile, preferred_element_type=F32).astype(BF)
    right_root = lax.dynamic_index_in_dim(right_stale[0], z, 0, keepdims=False)
    update = jnp.dot(applied, right_root, preferred_element_type=F32)
    return weight - 0.5 * update, new_stat[None, None], root[None, None]


def solution(mesh):
    split = Mesh(mesh.devices.reshape(4, 2, 4, 2, 2), ("z", "xl", "y", "xh", "core"))
    dp, mp = ("z", "xl"), ("y", "xh", "core")
    placed = (
        P(dp, mp),
        P(dp, mp),
        P(dp, mp),
        P(mp, dp, None, None),
        P(mp, dp),
        P(mp, dp, None),
        P(mp, None, None, None),
    )
    return jax.shard_map(
        on_device,
        mesh=split,
        in_specs=placed,
        out_specs=(P(dp, mp), P(mp, dp, None, None), P(mp, dp, None, None)),
        check_vma=False,
    )
```

```python
import jax
import jax.numpy as jnp
from jax import lax
from jax.experimental import pallas as pl
from jax.experimental.pallas import tpu as pltpu
from jax.sharding import Mesh, PartitionSpec as P

BLK = 1024
RB = 4
CHUNKS = 2
COLS = BLK // CHUNKS
ROWS = 256
BF = jnp.bfloat16
F32 = jnp.float32
MIB = 1024 * 1024
SWAP = [(0, 1), (1, 0)]


def ring(step):
    return [(i, (i + step) % 4) for i in range(4)]


def x_perm(pairs):
    def index(x):
        return (x % 2) * 2 + x // 2

    return [(index(s), index(d)) for s, d in pairs]


def after(value, *earlier):
    return lax.optimization_barrier((value,) + earlier)[0]


def add(first, *others):
    total = first.astype(F32)
    for other in others:
        total = total + other.astype(F32)
    return total.astype(BF)


def partial_kernel(z_ref, *refs):
    mine_cot, other_cot = refs[16], refs[17]
    out = refs[18]
    z = z_ref[0]
    for tile in range(4):
        place = lax.rem(tile - z + 8, 4)
        for part in range(2):
            mine = refs[tile * 4 + part * 2]
            other = refs[tile * 4 + part * 2 + 1]
            total = jnp.dot(mine[...], mine_cot[...], preferred_element_type=F32)
            total = total + jnp.dot(other[...], other_cot[...], preferred_element_type=F32)
            out[place, part * ROWS:(part + 1) * ROWS, :] = total.astype(BF)


def partial_product(z, pieces, mine_cot, other_cot):
    whole = pl.BlockSpec(memory_space=pltpu.VMEM)
    return pl.pallas_call(
        partial_kernel,
        out_shape=jax.ShapeDtypeStruct((4, 512, COLS), BF),
        in_specs=[pl.BlockSpec(memory_space=pltpu.SMEM)] + [whole] * 18,
        out_specs=whole,
        compiler_params=pltpu.CompilerParams(vmem_limit_bytes=24 * MIB),
        cost_estimate=pl.CostEstimate(flops=2 * 2048 * 2048 * COLS, bytes_accessed=12 << 20, transcendentals=0),
    )(jnp.reshape(z, (1,)).astype(jnp.int32), *pieces, mine_cot, other_cot)


def mm(left, right):
    return jnp.dot(left.astype(BF), right.astype(BF), preferred_element_type=F32)


def tail(problem, stat_prev, tile):
    oriented = jnp.where(problem < RB, tile, tile.T)
    gram = lax.dot_general(oriented, oriented, (((1,), (1,)), ((), ())), preferred_element_type=F32)
    stat = stat_prev + gram
    norm_scale = 2.0 * jnp.sum(stat * stat) / jnp.trace(stat)
    inverse = 1.0 / norm_scale
    m = stat * inverse
    m2 = mm(stat, stat) * (inverse * inverse)
    base = 25.0 / 16.0
    e = (m2 - 10.0 * m) * 0.0625
    mf = (5.0 * m - m2) * 0.25
    w = 2.0 * base * e + mm(e, e)
    rest = 6.25 * jnp.eye(BLK, dtype=F32) - 1.25 * m - (base * base) * mf
    return stat, (rest - mm(w, mf)) * (0.25 * norm_scale ** (-0.25))


def on_device(activations, cotangent, weight, stat_prev, assignment, left_stale, right_stale):
    z = lax.axis_index("z")
    xl = lax.axis_index("xl")
    y = lax.axis_index("y")
    xh = lax.axis_index("xh")
    core = lax.axis_index("core")
    half = xl ^ xh

    acts = lax.optimization_barrier(activations.T)
    other = lax.ppermute(acts, ("xl", "xh"), x_perm([(1, 0), (3, 2), (0, 3), (2, 1)]))
    acts2 = after(acts, other)
    recv_mine = lax.ppermute(acts2, ("xl", "xh"), x_perm([(1, 3), (3, 1)]))
    own_cots, other_cots = [], []
    previous = recv_mine
    for chunk in range(CHUNKS):
        own_cots.append(cotangent[:, chunk * COLS:(chunk + 1) * COLS])
        sent = after(own_cots[-1], previous)
        previous = lax.ppermute(sent, "xl", SWAP)
        other_cots.append(previous)
    mine = jnp.where(xl == 0, acts, recv_mine)

    other_below = lax.ppermute(other, "y", ring(1))
    other_above = lax.ppermute(other, "y", ring(-1))
    mine_below = lax.ppermute(mine, "y", ring(1))
    mine_above = lax.ppermute(mine, "y", ring(-1))
    mine_far = lax.ppermute(mine_below, "y", ring(1))
    other_far = lax.ppermute(other_above, "y", ring(-1))

    def core_swap(value):
        return lax.ppermute(value, "core", SWAP)

    pieces = []
    for pair in ((mine, other), (mine_above, other_above), (mine_far, other_far), (mine_below, other_below)):
        pieces += [pair[0], pair[1], core_swap(pair[0]), core_swap(pair[1])]

    problem = assignment[0, 0]
    partner_problem = lax.ppermute(assignment, "xl", SWAP)[0, 0]
    which = (problem % RB - z) % 4
    partner_which = (partner_problem % RB - z) % 4

    gathered, updates = [], []
    for chunk in range(CHUNKS):
        part = partial_product(z - y, pieces, own_cots[chunk], other_cots[chunk])
        up = lax.ppermute(part[2, :256], "z", ring(1))
        down = lax.ppermute(part[2, 256:], "z", ring(-1))
        nxt = jnp.concatenate([add(part[1, :256], up), part[1, 256:]], 0)
        prv = jnp.concatenate([part[3, :256], add(part[3, 256:], down)], 0)
        from_prv = lax.ppermute(nxt, "z", ring(1))
        from_nxt = lax.ppermute(prv, "z", ring(-1))
        own = add(part[0], from_prv, from_nxt)
        got_prv = lax.ppermute(own, "z", ring(1))
        got_nxt = lax.ppermute(own, "z", ring(-1))
        far_a = lax.ppermute(got_prv[:256], "z", ring(1))
        far_b = lax.ppermute(got_nxt[256:], "z", ring(-1))

        def pick(index):
            return lax.select_n(index, own, got_nxt, jnp.concatenate([far_a, far_b], 0), got_prv)

        gram_other = lax.ppermute(pick(partner_which), "xl", SWAP)
        gathered.append((pick(which), gram_other))
        updates.append((own, lax.ppermute(own, "xl", SWAP)))

    def assemble(pairs):
        sides = [jnp.concatenate([p[side] for p in pairs], 1) for side in range(2)]
        quarters = [sides[0][:ROWS], sides[0][ROWS:], sides[1][:ROWS], sides[1][ROWS:]]
        place = half * 2 + core
        return jnp.concatenate([lax.select_n(place, *[quarters[i ^ q] for q in range(4)]) for i in range(4)], 0)

    new_stat, root = tail(problem, stat_prev[0, 0], assemble(gathered))
    upd_tile = assemble(updates)
    applied = jnp.dot(left_stale[0], upd_tile, preferred_element_type=F32).astype(BF)
    right_root = lax.dynamic_index_in_dim(right_stale[0], z, 0, keepdims=False)
    update = jnp.dot(applied, right_root, preferred_element_type=F32)
    return weight - 0.5 * update, new_stat[None, None], root[None, None]


def solution(mesh):
    split = Mesh(mesh.devices.reshape(4, 2, 4, 2, 2), ("z", "xl", "y", "xh", "core"))
    dp, mp = ("z", "xl"), ("y", "xh", "core")
    placed = (
        P(dp, mp),
        P(dp, mp),
        P(dp, mp),
        P(mp, dp, None, None),
        P(mp, dp),
        P(mp, dp, None),
        P(mp, None, None, None),
    )
    return jax.shard_map(
        on_device,
        mesh=split,
        in_specs=placed,
        out_specs=(P(dp, mp), P(mp, dp, None, None), P(mp, dp, None, None)),
        check_vma=False,
    )
```
